512 devices in a mesh: seq: 16 (over x_lo, y, core), tp: 32 (over x_hi, z).
Axes of the slice: x: 4 (x_hi: 2, x_lo: 2; x = x_hi * 2 + x_lo), y: 4, z: 16, core: 2. Of those that a mesh axis runs over, the one named last changes fastest.
Arguments:
- tokens: bfloat16 [1024, 8192], P('tp', 'seq'), may hold values from -6 to 6
- cotangent: bfloat16 [1024, 8192], P('tp', 'seq'), may hold values from -0.5 to 0.5
- gate_codes: bfloat16 [8192, 16384], P('seq', 'tp'), may hold values from -4 to 4
- gate_scales: float32 [64, 128], replicated, may hold values from 0.004 to 0.02
- up_codes: bfloat16 [8192, 16384], P('seq', 'tp'), may hold values from -4 to 4
- up_scales: float32 [64, 128], replicated, may hold values from 0.004 to 0.02
- down_codes: bfloat16 [16384, 8192], P('tp', 'seq'), may hold values from -4 to 4
- down_scales: float32 [128, 64], replicated, may hold values from 0.004 to 0.02
Outputs:
- mixed_out: bfloat16 [1024, 8192], P('tp', 'seq')
- grad_gate: float32 [8192, 16384], P('seq', 'tp')
- grad_up: float32 [8192, 16384], P('seq', 'tp')
- grad_down: float32 [16384, 8192], P('tp', 'seq')
The draws below stay inside these ranges and needn't reach their ends.
All inputs are finite; a program needn't handle non-finite values.
Results may differ from the reference program's by a relative error of at most 0.04.
Values may be sent and summed in bfloat16 or wider, within the bound.
No kernel may reach another device: no remote copies, remote signals or barrier semaphores. Data moves between devices by JAX's collectives and lax.ppermute only.
A program may use at most 64 MiB of HBM per device.

```python
import math
import jax
import jax.numpy as jnp
from jax import lax

D = 8192
FF = 16384
BLOCK = 128
TOKENS = 1024
N_SEQ = 16
N_TP = 32


def block_levels(rng, dims, shards, low, top_value):
    gain, own = 1.0, jax.random.fold_in(rng, 6)
    for dim, parts in shards:
        steps = jnp.exp(jax.random.uniform(jax.random.fold_in(own, dim), (parts,), jnp.float32, low / len(shards), top_value / len(shards)))
        gain = gain * jnp.repeat(steps, dims[dim] // parts).reshape([-1 if axis == dim else 1 for axis in range(len(dims))])
    return gain


def gaussian(own_key, shape, scale, bound, split=(), dtype=jnp.bfloat16):
    factor_of = block_levels(own_key, shape, split, -0.22, 0.18) if split else 1.0
    result = jax.random.normal(own_key, shape, jnp.float32) * scale * factor_of
    return jnp.minimum(jnp.maximum(result, -bound), bound).astype(dtype)


def setup_inputs(seed: int = 0) -> dict:
    key_of = jax.random.split(jax.random.key(seed), 9)
    return {
        "tokens": gaussian(key_of[0], (TOKENS, D), 1.0, 6.0, ((0, 32), (1, 16))),
        "cotangent": gaussian(key_of[1], (TOKENS, D), 0.0625, 0.5, ((0, 32), (1, 16))),
        "gate_codes": gaussian(key_of[2], (D, FF), 1.0, 4.0, ((0, 16), (1, 32))),
        "gate_scales": jnp.clip(jnp.exp(jax.random.uniform(key_of[3], (D // BLOCK, FF // BLOCK), jnp.float32, math.log(0.004), math.log(0.02))), 0.004, 0.02),
        "up_codes": gaussian(key_of[4], (D, FF), 1.0, 4.0, ((0, 16), (1, 32))),
        "up_scales": jnp.clip(jnp.exp(jax.random.uniform(key_of[5], (D // BLOCK, FF // BLOCK), jnp.float32, math.log(0.004), math.log(0.02))), 0.004, 0.02),
        "down_codes": gaussian(key_of[6], (FF, D), 1.0, 4.0, ((0, 32), (1, 16))),
        "down_scales": jnp.clip(jnp.exp(jax.random.uniform(key_of[7], (FF // BLOCK, D // BLOCK), jnp.float32, math.log(0.004), math.log(0.02))), 0.004, 0.02),
    }


def expand_scales(scales):
    return jnp.repeat(jnp.repeat(scales, BLOCK, axis=0), BLOCK, axis=1)


def dequantize(codes, scales):
    return (codes.astype(jnp.float32) * expand_scales(scales)).astype(jnp.bfloat16)


def rounded_term(left, right):
    term = jnp.dot(left, right, preferred_element_type=jnp.float32)
    return lax.optimization_barrier(term.astype(jnp.bfloat16)).astype(jnp.float32)


def reference(tokens, cotangent, gate_codes, gate_scales, up_codes, up_scales, down_codes, down_scales):
    w_gate = dequantize(gate_codes, gate_scales)
    w_up = dequantize(up_codes, up_scales)
    w_down = dequantize(down_codes, down_scales)
    width_rows = D // N_SEQ
    unit_cols = FF // N_TP
    w_pair = jnp.concatenate([w_gate, w_up], axis=1)
    totals = jnp.zeros((TOKENS, 2 * FF), jnp.float32)
    for block_index in range(N_SEQ):
        lower = block_index * width_rows
        totals = totals + rounded_term(tokens[:, lower:lower + width_rows], w_pair[lower:lower + width_rows])
    gate_sum = totals[:, :FF]
    up_sum = totals[:, FF:]
    hidden = (jax.nn.silu(gate_sum) * up_sum).astype(jnp.bfloat16)
    output_total = jnp.zeros((TOKENS, D), jnp.float32)
    for block_index in range(N_TP):
        lower = block_index * unit_cols
        output_total = output_total + rounded_term(hidden[:, lower:lower + unit_cols], w_down[lower:lower + unit_cols])
    mixed_out = output_total.astype(jnp.bfloat16)
    hidden_grad = jnp.zeros((TOKENS, FF), jnp.float32)
    for block_index in range(N_SEQ):
        lower = block_index * width_rows
        hidden_grad = hidden_grad + rounded_term(cotangent[:, lower:lower + width_rows], w_down[:, lower:lower + width_rows].T)
    sigma = jax.nn.sigmoid(gate_sum)
    gate_grad = (hidden_grad * up_sum * sigma * (1.0 + gate_sum * (1.0 - sigma))).astype(jnp.bfloat16)
    up_grad = (hidden_grad * jax.nn.silu(gate_sum)).astype(jnp.bfloat16)
    grad_gate = jnp.dot(tokens.T, gate_grad, preferred_element_type=jnp.float32)
    grad_up = jnp.dot(tokens.T, up_grad, preferred_element_type=jnp.float32)
    grad_down = jnp.dot(hidden.T, cotangent, preferred_element_type=jnp.float32)
    return mixed_out, grad_gate, grad_up, grad_down
```

```python
import jax
import jax.numpy as jnp
from jax import lax
from jax.experimental import pallas as pl
from jax.experimental.pallas import tpu as pltpu
from jax.sharding import Mesh, PartitionSpec as P

BLOCK = 128
F32 = jnp.float32
BF16 = jnp.bfloat16

SEQ = ("xl", "y", "core")
PLANE = ("xl", "y")
Z = ("zh", "zl")
TP = ("xh", "zh", "zl")
SIZES = (2, 4, 2, 2, 4, 4)


def dequantize(codes, scales, row_place, col_place):
    rows, cols = codes.shape
    up, across = rows // BLOCK, cols // BLOCK
    picked = lax.dynamic_slice(scales, (row_place * up, col_place * across), (up, across))
    factors = jnp.broadcast_to(picked[:, None, :, None], (up, BLOCK, across, BLOCK))
    return (codes.astype(F32) * factors.reshape(rows, cols)).astype(BF16)


def shift(x, axes, size, by):
    return lax.ppermute(x, axes, [(i, (i + by) % size) for i in range(size)])


def other_core(x):
    return shift(x, "core", 2, 1)


def other_xh(x):
    return shift(x, "xh", 2, 1)


def pick(x, place):
    return lax.dynamic_index_in_dim(x, place, 0, keepdims=False)


def dot(a, b):
    return jnp.dot(a, b, preferred_element_type=F32)


def dot_nt(a, b):
    return lax.dot_general(a, b, (((1,), (1,)), ((), ())), preferred_element_type=F32)


def dot_tn(a, b):
    return lax.dot_general(a, b, (((0,), (0,)), ((), ())), preferred_element_type=F32)


def summed(x, axes):
    return lax.all_to_all(x, axes, 0, 0, tiled=False).astype(F32).sum(0)


def spread(x, count):
    copies = jnp.broadcast_to(x[None], (count,) + x.shape)
    return lax.all_to_all(copies, PLANE, 0, 0, tiled=False)


def forward_kernel(frames, near, far, near_other, far_other, out):
    width, units = near.shape[1], near.shape[2]
    own, swap = frames[:, :width], frames[:, width:]
    out[:, :units] = (dot(own, near[0]) + dot(swap, near_other[0])).astype(BF16)
    out[:, units:] = (dot(own, far[0]) + dot(swap, far_other[0])).astype(BF16)


def back_kernel(frames, near, far, near_other, far_other, out):
    width, units = near.shape[2], near.shape[1]
    own, swap = frames[:, :width], frames[:, width:]
    out[:, :units] = (dot_nt(own, near[0]) + dot_nt(swap, near_other[0])).astype(BF16)
    out[:, units:] = (dot_nt(own, far[0]) + dot_nt(swap, far_other[0])).astype(BF16)


def parts_call(kernel, name, first, count, frames, weights):
    _, width, units = weights[0].shape
    rows = frames.shape[0]
    weight = pl.BlockSpec((1, width, units), lambda k: (k + first, 0, 0))
    return pl.pallas_call(
        kernel,
        grid=(count,),
        in_specs=[pl.BlockSpec(frames.shape, lambda k: (0, 0))] + [weight] * 4,
        out_specs=pl.BlockSpec((rows, 2 * units), lambda k: (0, k)),
        out_shape=jax.ShapeDtypeStruct((rows, 2 * units * count), BF16),
        compiler_params=pltpu.CompilerParams(vmem_limit_bytes=32 * 1024 * 1024),
        cost_estimate=pl.CostEstimate(
            flops=count * 8 * rows * width * units,
            bytes_accessed=count * (8 * width * units + 4 * rows * units) + 4 * rows * width,
            transcendentals=0,
        ),
        name=name,
    )(frames, *weights)


def forward_parts(frames, weights):
    return parts_call(forward_kernel, "forward_parts", 0, 2, frames, weights)


def back_parts(frames, weights):
    return parts_call(back_kernel, "back_parts", 2, 1, frames, weights)


def on_device(
    tokens, cotangent, gate_codes, gate_scales, up_codes, up_scales, down_codes, down_scales
):
    seq_place = lax.axis_index(SEQ)
    tp_place = lax.axis_index(TP)
    core = lax.axis_index("core")
    rows, width = tokens.shape
    units = gate_codes.shape[1]
    half = rows // 2
    quarter = 16 * half

    w_near = jnp.stack(
        [
            dequantize(gate_codes, gate_scales, seq_place, tp_place),
            dequantize(up_codes, up_scales, seq_place, tp_place),
            dequantize(down_codes, down_scales, tp_place, seq_place),
        ]
    )
    w_near, tokens, cotangent = lax.optimization_barrier((w_near, tokens, cotangent))
    w_far = other_xh(w_near)
    w_near_other = other_core(w_near)

    halves = jnp.stack([tokens.reshape(2, half, width), cotangent.reshape(2, half, width)], axis=1)
    kept, got = pick(halves, core), other_core(pick(halves, 1 - core))
    mine = jnp.concatenate([kept, got], axis=2)
    frames = lax.all_gather(mine[0], Z, axis=0, tiled=True)
    w_far, frames = lax.optimization_barrier((w_far, frames))
    w_far_other = other_core(w_far)
    weights = (w_near, w_far, w_near_other, w_far_other)

    parts = forward_parts(frames, weights)
    parts, grads_mine = lax.optimization_barrier((parts, mine[1]))
    totals = summed(parts.reshape(8, rows, 4 * units), PLANE)
    grads_in = lax.all_gather(grads_mine, Z, axis=0, tiled=True)
    gate_sum = totals[:, : 2 * units]
    up_sum = totals[:, 2 * units :]
    sigma = jax.nn.sigmoid(gate_sum)
    silu = gate_sum * sigma
    hidden = (silu * up_sum).astype(BF16)

    back = back_parts(grads_in, weights)
    frames, back, grads_in = lax.optimization_barrier((frames, back, grads_in))
    both = jnp.concatenate(
        [jnp.broadcast_to(hidden[None], (8, rows, 2 * units)), back.reshape(8, rows, 2 * units)], axis=2
    )
    both = lax.all_to_all(both, PLANE, 0, 0, tiled=False)
    hidden_grad = both[:, :, 2 * units :].astype(F32).sum(0)
    gate_grad = (hidden_grad * up_sum * sigma * (1.0 + gate_sum * (1.0 - sigma))).astype(BF16)
    up_grad = (hidden_grad * silu).astype(BF16)

    hidden_own = both[:, :, : 2 * units].reshape(quarter, 2 * units)
    hidden_other = other_core(hidden_own)
    w_down_pair = jnp.concatenate([w_near[2], w_far[2]])
    mixed = jnp.stack(
        [dot(hidden_own, w_down_pair).astype(BF16), dot(hidden_other, w_down_pair).astype(BF16)]
    )
    mixed = mixed.reshape(2, 16, half, width).transpose(1, 0, 2, 3)

    kept = jnp.concatenate([gate_grad[:, :units], up_grad[:, :units]], axis=1)
    sent = jnp.concatenate([gate_grad[:, units:], up_grad[:, units:]], axis=1)
    grads_own = spread(jnp.stack([kept, other_xh(sent)]), 8).reshape(8, 2, rows, 2 * units)

    swap = other_core(jnp.concatenate([frames[:, width:], grads_in[:, width:]], axis=1))
    near = jnp.concatenate([frames[:, :width], grads_in[:, :width]], axis=1)
    near, swap = lax.optimization_barrier((near, swap))
    far = other_xh(jnp.concatenate([near, swap]))
    units_far = other_xh(jnp.concatenate([hidden_own[:, units:], hidden_other[:, units:]]))

    grads_own, mixed = lax.optimization_barrier((grads_own, mixed))
    grads_other = other_core(grads_own)
    mixed = summed(mixed, Z)
    mixed = jnp.where(core == 0, mixed, mixed[::-1]).astype(BF16).reshape(rows, width)
    mixed, far, units_far = lax.optimization_barrier((mixed, far, units_far))

    def over_frames(near, swap, far, near_right, swap_right, far_right):
        return dot_tn(near, near_right) + dot_tn(swap, swap_right) + dot_tn(far, far_right)

    flat = lambda x, place, part: x[:, place].reshape(quarter, 2 * units)[:, part]

    def pair_grad(part):
        return over_frames(
            near[:, :width],
            swap[:, :width],
            far[:, :width],
            flat(grads_own, 0, part),
            flat(grads_other, 0, part),
            jnp.concatenate([flat(grads_own, 1, part), flat(grads_other, 1, part)]),
        )

    grad_gate, grad_up = pair_grad(slice(0, units)), pair_grad(slice(units, 2 * units))
    grad_down = over_frames(
        hidden_own[:, :units],
        hidden_other[:, :units],
        units_far,
        near[:, width:],
        swap[:, width:],
        far[:, width:],
    )
    return (mixed, grad_gate, grad_up, grad_down)


def solution(mesh):
    named = Mesh(mesh.devices.reshape(SIZES), SEQ + TP)
    return jax.shard_map(
        on_device,
        mesh=named,
        in_specs=(
            P(TP, SEQ),
            P(TP, SEQ),
            P(SEQ, TP),
            P(),
            P(SEQ, TP),
            P(),
            P(TP, SEQ),
            P(),
        ),
        out_specs=(P(TP, SEQ), P(SEQ, TP), P(SEQ, TP), P(TP, SEQ)),
        check_vma=False,
    )
```

```python
import jax
import jax.numpy as jnp
from jax import lax
from jax.experimental import pallas as pl
from jax.experimental.pallas import tpu as pltpu
from jax.sharding import Mesh, PartitionSpec as P

BLOCK = 128
LANES = 128
F32 = jnp.float32
BF16 = jnp.bfloat16

SEQ = ("xl", "y", "core")
PLANE = ("xl", "y")
Z = ("zh", "zm", "zn")
TP = ("xh", "zh", "zm", "zn")
SIZES = (2, 4, 2, 2, 4, 2, 2)


def dequantize_kernel(place, gate_scales, up_scales, down_scales, gate, up, down, out):
    low, turn = place[0] % 2 == 0, (LANES - 4 * place[1]) % LANES
    for kind, (codes, scales) in enumerate(((gate, gate_scales), (up, up_scales), (down, down_scales))):
        factors = pltpu.roll(jnp.where(low, scales[:4], scales[4:]), turn, 1)
        for w in range(4):
            for u in range(4):
                r, c = (u, w) if kind == 2 else (w, u)
                rows, cols = slice(r * BLOCK, (r + 1) * BLOCK), slice(c * BLOCK, (c + 1) * BLOCK)
                factor = jnp.broadcast_to(factors[w : w + 1, u : u + 1], (BLOCK, BLOCK))
                out[kind, rows, cols] = (codes[rows, cols].astype(F32) * factor).astype(BF16)


def dequantize(place, codes, scales):
    size = codes[0].shape
    scale = pl.BlockSpec((8, LANES), lambda i, place: (place[0] // 2, 0))
    return pl.pallas_call(
        dequantize_kernel,
        grid_spec=pltpu.PrefetchScalarGridSpec(
            num_scalar_prefetch=1,
            grid=(1,),
            in_specs=[scale] * 3 + [pl.BlockSpec(size, lambda i, place: (0, 0))] * 3,
            out_specs=pl.BlockSpec((3,) + size, lambda i, place: (0, 0, 0)),
        ),
        out_shape=jax.ShapeDtypeStruct((3,) + size, BF16),
        compiler_params=pltpu.CompilerParams(vmem_limit_bytes=56 * 1024 * 1024),
        name="dequantize",
    )(place, *scales, *codes)


def shift(x, axes, size, by):
    return lax.ppermute(x, axes, [(i, (i + by) % size) for i in range(size)])


def other_core(x):
    return shift(x, "core", 2, 1)


def other_xh(x):
    return shift(x, "xh", 2, 1)


def pick(x, place):
    return lax.dynamic_index_in_dim(x, place, 0, keepdims=False)


def dot(a, b):
    return jnp.dot(a, b, preferred_element_type=F32)


def dot_nt(a, b):
    return lax.dot_general(a, b, (((1,), (1,)), ((), ())), preferred_element_type=F32)


def dot_tn(a, b):
    return lax.dot_general(a, b, (((0,), (0,)), ((), ())), preferred_element_type=F32)


def summed(x, axes):
    return lax.all_to_all(x, axes, 0, 0, tiled=False).astype(F32).sum(0)


def halved(x, place, pairs):
    x = x.reshape((x.shape[0] // 2, 2) + x.shape[1:])
    own, away = (lax.dynamic_index_in_dim(x, p, 1, keepdims=False) for p in (place, 1 - place))
    return (own.astype(F32) + lax.ppermute(away, Z, pairs).astype(F32)).astype(BF16)


def spread(x, count):
    copies = jnp.broadcast_to(x[None], (count,) + x.shape)
    return lax.all_to_all(copies, PLANE, 0, 0, tiled=False)


def forward_kernel(frames, tail, near, far, near_other, far_other, out):
    width, units = near.shape[1], near.shape[2]
    kind = pl.program_id(0)

    @pl.when(kind < 2)
    def _():
        own, swap = frames[:, :width], frames[:, width : 2 * width]
        out[:, :units] = (dot(own, near[0]) + dot(swap, near_other[0])).astype(BF16)
        out[:, units:] = (dot(own, far[0]) + dot(swap, far_other[0])).astype(BF16)

    @pl.when(kind == 2)
    def _():
        own = frames[:, 2 * width : 3 * width]
        swap = jnp.concatenate([frames[:, 3 * width :], tail[...]], axis=1)
        out[:, :units] = (dot_nt(own, near[0]) + dot_nt(swap, near_other[0])).astype(BF16)
        out[:, units:] = (dot_nt(own, far[0]) + dot_nt(swap, far_other[0])).astype(BF16)


def forward_parts(frames, tail, near, far, near_other, far_other):
    count, width, units = near.shape
    whole = lambda x: pl.BlockSpec(x.shape, lambda k: (0, 0))
    weight = pl.BlockSpec((1, width, units), lambda k: (k, 0, 0))
    return pl.pallas_call(
        forward_kernel,
        grid=(count,),
        in_specs=[whole(frames), whole(tail), weight, weight, weight, weight],
        out_specs=pl.BlockSpec((frames.shape[0], 2 * units), lambda k: (0, k)),
        out_shape=jax.ShapeDtypeStruct((frames.shape[0], 2 * units * count), BF16),
        compiler_params=pltpu.CompilerParams(vmem_limit_bytes=32 * 1024 * 1024),
        cost_estimate=pl.CostEstimate(flops=12 * frames.shape[0] * 2 * width * units, bytes_accessed=12 * width * units * 2 + 6 * frames.shape[0] * units * 2, transcendentals=0),
        name="forward_parts",
    )(frames, tail, near, far, near_other, far_other)


def plane_kernel(arrived, hidden, kept, sent):
    units = arrived.shape[2] // 6
    places = arrived.shape[0]
    total = arrived[0].astype(F32)
    for place in range(1, places):
        total = total + arrived[place].astype(F32)
    gate_sum, up_sum, hidden_grad = (total[:, 2 * k * units : 2 * (k + 1) * units] for k in range(3))
    sigma = jax.nn.sigmoid(gate_sum)
    silu = gate_sum * sigma
    out = (silu * up_sum).astype(BF16)
    for place in range(places):
        hidden[place] = out
    gate_grad = (hidden_grad * up_sum * sigma * (1.0 + gate_sum * (1.0 - sigma))).astype(BF16)
    up_grad = (hidden_grad * silu).astype(BF16)
    kept[:, :units], kept[:, units:] = gate_grad[:, :units], up_grad[:, :units]
    sent[:, :units], sent[:, units:] = gate_grad[:, units:], up_grad[:, units:]


def plane_parts(arrived):
    places, rows, columns = arrived.shape
    shapes = [(places, rows, columns // 3), (rows, columns // 3), (rows, columns // 3)]
    whole = lambda shape: pl.BlockSpec(shape, lambda i: (0,) * len(shape))
    return pl.pallas_call(
        plane_kernel,
        grid=(1,),
        in_specs=[whole(arrived.shape)],
        out_specs=[whole(shape) for shape in shapes],
        out_shape=[jax.ShapeDtypeStruct(shape, BF16) for shape in shapes],
        compiler_params=pltpu.CompilerParams(vmem_limit_bytes=32 * 1024 * 1024),
        name="plane_parts",
    )(arrived)


def pair_kernel(token_pair, token_far, own, other, gate, up):
    quarter, units = token_pair.shape[0] // 2, gate.shape[1]

    def product(columns):
        total = None
        for core, grads in enumerate((own, other)):
            for x_hi, tokens in enumerate((token_pair, token_far)):
                right = grads[:, x_hi, :, columns].reshape(quarter, units)
                term = dot_tn(tokens[core * quarter : (core + 1) * quarter], right)
                total = term if total is None else total + term
        return total

    gate[...] = product(slice(0, units))
    up[...] = product(slice(units, 2 * units))


def pair_grads(token_pair, token_far, own, other):
    width, units = token_pair.shape[1], own.shape[3] // 2
    step = width // 2
    tokens = pl.BlockSpec((token_pair.shape[0], step), lambda i: (0, i))
    grads = pl.BlockSpec(own.shape, lambda i: (0, 0, 0, 0))
    return pl.pallas_call(
        pair_kernel,
        grid=(2,),
        in_specs=[tokens, tokens, grads, grads],
        out_specs=[pl.BlockSpec((step, units), lambda i: (i, 0))] * 2,
        out_shape=[jax.ShapeDtypeStruct((width, units), F32)] * 2,
        compiler_params=pltpu.CompilerParams(vmem_limit_bytes=32 * 1024 * 1024),
        cost_estimate=pl.CostEstimate(
            flops=8 * token_pair.shape[0] * width * units,
            bytes_accessed=4 * token_pair.shape[0] * (width + 2 * units) + 8 * width * units,
            transcendentals=0,
        ),
        name="pair_grads",
    )(token_pair, token_far, own, other)


def on_device(
    tokens, cotangent, gate_codes, gate_scales, up_codes, up_scales, down_codes, down_scales
):
    seq_place = lax.axis_index(SEQ)
    tp_place = lax.axis_index(TP)
    core = lax.axis_index("core")
    rows, width = tokens.shape
    units = gate_codes.shape[1]
    half = rows // 2
    quarter = 16 * half

    place = jnp.stack([seq_place, tp_place]).astype(jnp.int32)
    w_near = dequantize(
        place, (gate_codes, up_codes, down_codes), (gate_scales, up_scales, down_scales.T)
    )
    w_near, tokens, cotangent = lax.optimization_barrier((w_near, tokens, cotangent))
    w_far = other_xh(w_near)
    w_near_other = other_core(w_near)

    halves = jnp.stack([tokens.reshape(2, half, width), cotangent.reshape(2, half, width)], axis=1)
    kept, got = pick(halves, core), other_core(pick(halves, 1 - core))
    mine = jnp.concatenate([kept[0], got[0], kept[1], got[1]], axis=1)
    body = 4 * width - LANES
    tail = lax.all_to_all(jnp.broadcast_to(mine[None, :, body:], (16, half, LANES)), Z, 0, 0, tiled=False)
    tail = tail.reshape(quarter, LANES)
    frames = lax.all_gather(mine[:, :body], Z, axis=0, tiled=True)
    w_far, frames, tail = lax.optimization_barrier((w_far, frames, tail))
    w_far_other = other_core(w_far)

    parts = forward_parts(frames, tail, w_near, w_far, w_near_other, w_far_other)
    parts, frames, tail = lax.optimization_barrier((parts, frames, tail))
    arrived = lax.all_to_all(parts.reshape(8, rows, 6 * units), PLANE, 0, 0, tiled=False)

    swap = other_core(jnp.concatenate([frames[:, width : 2 * width], frames[:, 3 * width :], tail], axis=1))
    token_pair = jnp.concatenate([frames[:, :width], swap[:, :width]])
    cot_pair = jnp.concatenate([frames[:, 2 * width : 3 * width], swap[:, width:]])
    hidden, kept, sent = plane_parts(arrived)
    hidden_own = lax.all_to_all(hidden, PLANE, 0, 0, tiled=False)

    got, hidden_own, token_far = lax.optimization_barrier((other_xh(sent), hidden_own, other_xh(token_pair)))
    grads_own = spread(jnp.stack([kept, got]), 8).reshape(8, 2, rows, 2 * units)

    hidden_own = hidden_own.reshape(quarter, 2 * units)
    hidden_other = other_core(hidden_own)
    w_down_pair = jnp.concatenate([w_near[2], w_far[2]])
    mixed = jnp.stack(
        [dot(hidden_own, w_down_pair).astype(BF16), dot(hidden_other, w_down_pair).astype(BF16)]
    )
    mixed = mixed.reshape(2, 16, half, width).transpose(1, 0, 2, 3).reshape(16, rows, width)
    mixed = halved(mixed, lax.axis_index("zn"), [(i, i ^ 1) for i in range(16)])
    units_pair = jnp.concatenate([hidden_own[:, :units], hidden_other[:, :units]])
    units_far = other_xh(jnp.concatenate([hidden_own[:, units:], hidden_other[:, units:]]))
    grads_own, mixed, cot_pair, units_far = lax.optimization_barrier((grads_own, mixed, cot_pair, units_far))
    cot_far = other_xh(cot_pair)
    grads_other = other_core(grads_own)
    mixed = summed(mixed, ("zh", "zm")).reshape(2, half, width)
    mixed = jnp.where(core == 0, mixed, mixed[::-1]).astype(BF16).reshape(rows, width)

    mixed, cot_far = lax.optimization_barrier((mixed, cot_far))

    grad_gate, grad_up = pair_grads(token_pair, token_far, grads_own, grads_other)
    grad_down = dot_tn(units_pair, cot_pair) + dot_tn(units_far, cot_far)
    return (mixed, grad_gate, grad_up, grad_down)


def solution(mesh):
    named = Mesh(mesh.devices.reshape(SIZES), SEQ + TP)
    return jax.shard_map(
        on_device,
        mesh=named,
        in_specs=(
            P(TP, SEQ),
            P(TP, SEQ),
            P(SEQ, TP),
            P(),
            P(SEQ, TP),
            P(),
            P(TP, SEQ),
            P(),
        ),
        out_specs=(P(TP, SEQ), P(SEQ, TP), P(SEQ, TP), P(TP, SEQ)),
        check_vma=False,
    )
```

```python
import jax
import jax.numpy as jnp
from jax import lax
from jax.experimental import pallas as pl
from jax.experimental.pallas import tpu as pltpu
from jax.sharding import Mesh, PartitionSpec as P

BLOCK = 128
LANES = 128
F32 = jnp.float32
BF16 = jnp.bfloat16

SEQ = ("xl", "y", "core")
PLANE = ("xl", "y")
Z = ("zh", "zm", "zn")
TP = ("xh", "zh", "zm", "zn")
SIZES = (2, 4, 2, 2, 4, 2, 2)


def dequantize_kernel(place, gate_scales, up_scales, down_scales, gate, up, down, out):
    low, turn = place[0] % 2 == 0, (LANES - 4 * place[1]) % LANES
    for kind, (codes, scales) in enumerate(((gate, gate_scales), (up, up_scales), (down, down_scales))):
        factors = pltpu.roll(jnp.where(low, scales[:4], scales[4:]), turn, 1)
        for w in range(4):
            for u in range(4):
                r, c = (u, w) if kind == 2 else (w, u)
                rows, cols = slice(r * BLOCK, (r + 1) * BLOCK), slice(c * BLOCK, (c + 1) * BLOCK)
                factor = jnp.broadcast_to(factors[w : w + 1, u : u + 1], (BLOCK, BLOCK))
                out[kind, rows, cols] = (codes[rows, cols].astype(F32) * factor).astype(BF16)


def dequantize(place, codes, scales):
    size = codes[0].shape
    scale = pl.BlockSpec((8, LANES), lambda i, place: (place[0] // 2, 0))
    return pl.pallas_call(
        dequantize_kernel,
        grid_spec=pltpu.PrefetchScalarGridSpec(
            num_scalar_prefetch=1,
            grid=(1,),
            in_specs=[scale] * 3 + [pl.BlockSpec(size, lambda i, place: (0, 0))] * 3,
            out_specs=pl.BlockSpec((3,) + size, lambda i, place: (0, 0, 0)),
        ),
        out_shape=jax.ShapeDtypeStruct((3,) + size, BF16),
        compiler_params=pltpu.CompilerParams(vmem_limit_bytes=56 * 1024 * 1024),
        name="dequantize",
    )(place, *scales, *codes)


def shift(x, axes, size, by):
    return lax.ppermute(x, axes, [(i, (i + by) % size) for i in range(size)])


def other_core(x):
    return shift(x, "core", 2, 1)


def other_xh(x):
    return shift(x, "xh", 2, 1)


def pick(x, place):
    return lax.dynamic_index_in_dim(x, place, 0, keepdims=False)


def dot(a, b):
    return jnp.dot(a, b, preferred_element_type=F32)


def dot_nt(a, b):
    return lax.dot_general(a, b, (((1,), (1,)), ((), ())), preferred_element_type=F32)


def dot_tn(a, b):
    return lax.dot_general(a, b, (((0,), (0,)), ((), ())), preferred_element_type=F32)


def halved(x, place, pairs):
    x = x.reshape((x.shape[0] // 2, 2) + x.shape[1:])
    own, away = (lax.dynamic_index_in_dim(x, p, 1, keepdims=False) for p in (place, 1 - place))
    return (own.astype(F32) + lax.ppermute(away, Z, pairs).astype(F32)).astype(BF16)


def spread(x, count):
    copies = jnp.broadcast_to(x[None], (count,) + x.shape)
    return lax.all_to_all(copies, PLANE, 0, 0, tiled=False)


def forward_kernel(frames, tail, near, far, near_other, far_other, out):
    width, units = near.shape[1], near.shape[2]
    kind = pl.program_id(0)

    @pl.when(kind < 2)
    def _():
        own, swap = frames[:, :width], frames[:, width : 2 * width]
        out[:, :units] = (dot(own, near[0]) + dot(swap, near_other[0])).astype(BF16)
        out[:, units:] = (dot(own, far[0]) + dot(swap, far_other[0])).astype(BF16)

    @pl.when(kind == 2)
    def _():
        own = frames[:, 2 * width : 3 * width]
        swap = jnp.concatenate([frames[:, 3 * width :], tail[...]], axis=1)
        out[:, :units] = (dot_nt(own, near[0]) + dot_nt(swap, near_other[0])).astype(BF16)
        out[:, units:] = (dot_nt(own, far[0]) + dot_nt(swap, far_other[0])).astype(BF16)


def forward_parts(frames, tail, near, far, near_other, far_other):
    count, width, units = near.shape
    whole = lambda x: pl.BlockSpec(x.shape, lambda k: (0, 0))
    weight = pl.BlockSpec((1, width, units), lambda k: (k, 0, 0))
    return pl.pallas_call(
        forward_kernel,
        grid=(count,),
        in_specs=[whole(frames), whole(tail), weight, weight, weight, weight],
        out_specs=pl.BlockSpec((frames.shape[0], 2 * units), lambda k: (0, k)),
        out_shape=jax.ShapeDtypeStruct((frames.shape[0], 2 * units * count), BF16),
        compiler_params=pltpu.CompilerParams(vmem_limit_bytes=32 * 1024 * 1024),
        cost_estimate=pl.CostEstimate(flops=12 * frames.shape[0] * 2 * width * units, bytes_accessed=12 * width * units * 2 + 6 * frames.shape[0] * units * 2, transcendentals=0),
        name="forward_parts",
    )(frames, tail, near, far, near_other, far_other)


def plane_kernel(arrived, hidden, kept, sent):
    units = arrived.shape[2] // 6
    places = arrived.shape[0]
    total = arrived[0].astype(F32)
    for place in range(1, places):
        total = total + arrived[place].astype(F32)
    gate_sum, up_sum, hidden_grad = (total[:, 2 * k * units : 2 * (k + 1) * units] for k in range(3))
    sigma = jax.nn.sigmoid(gate_sum)
    silu = gate_sum * sigma
    out = (silu * up_sum).astype(BF16)
    for place in range(places):
        hidden[place] = out
    gate_grad = (hidden_grad * up_sum * sigma * (1.0 + gate_sum * (1.0 - sigma))).astype(BF16)
    up_grad = (hidden_grad * silu).astype(BF16)
    kept[:, :units], kept[:, units:] = gate_grad[:, :units], up_grad[:, :units]
    sent[:, :units], sent[:, units:] = gate_grad[:, units:], up_grad[:, units:]


def plane_parts(arrived):
    places, rows, columns = arrived.shape
    shapes = [(places, rows, columns // 3), (rows, columns // 3), (rows, columns // 3)]
    whole = lambda shape: pl.BlockSpec(shape, lambda i: (0,) * len(shape))
    return pl.pallas_call(
        plane_kernel,
        grid=(1,),
        in_specs=[whole(arrived.shape)],
        out_specs=[whole(shape) for shape in shapes],
        out_shape=[jax.ShapeDtypeStruct(shape, BF16) for shape in shapes],
        compiler_params=pltpu.CompilerParams(vmem_limit_bytes=32 * 1024 * 1024),
        name="plane_parts",
    )(arrived)


def pair_kernel(token_pair, token_far, own, other, gate, up):
    quarter, units = token_pair.shape[0] // 2, gate.shape[1]

    def product(columns):
        total = None
        for core, grads in enumerate((own, other)):
            for x_hi, tokens in enumerate((token_pair, token_far)):
                right = grads[:, x_hi, :, columns].reshape(quarter, units)
                term = dot_tn(tokens[core * quarter : (core + 1) * quarter], right)
                total = term if total is None else total + term
        return total

    gate[...] = product(slice(0, units))
    up[...] = product(slice(units, 2 * units))


def pair_grads(token_pair, token_far, own, other):
    width, units = token_pair.shape[1], own.shape[3] // 2
    step = width // 2
    tokens = pl.BlockSpec((token_pair.shape[0], step), lambda i: (0, i))
    grads = pl.BlockSpec(own.shape, lambda i: (0, 0, 0, 0))
    return pl.pallas_call(
        pair_kernel,
        grid=(2,),
        in_specs=[tokens, tokens, grads, grads],
        out_specs=[pl.BlockSpec((step, units), lambda i: (i, 0))] * 2,
        out_shape=[jax.ShapeDtypeStruct((width, units), F32)] * 2,
        compiler_params=pltpu.CompilerParams(vmem_limit_bytes=32 * 1024 * 1024),
        cost_estimate=pl.CostEstimate(
            flops=8 * token_pair.shape[0] * width * units,
            bytes_accessed=4 * token_pair.shape[0] * (width + 2 * units) + 8 * width * units,
            transcendentals=0,
        ),
        name="pair_grads",
    )(token_pair, token_far, own, other)


def on_device(
    tokens, cotangent, gate_codes, gate_scales, up_codes, up_scales, down_codes, down_scales
):
    seq_place = lax.axis_index(SEQ)
    tp_place = lax.axis_index(TP)
    core = lax.axis_index("core")
    rows, width = tokens.shape
    units = gate_codes.shape[1]
    half = rows // 2
    quarter = 16 * half

    place = jnp.stack([seq_place, tp_place]).astype(jnp.int32)
    w_near = dequantize(
        place, (gate_codes, up_codes, down_codes), (gate_scales, up_scales, down_scales.T)
    )
    w_near, tokens, cotangent = lax.optimization_barrier((w_near, tokens, cotangent))
    w_far = other_xh(w_near)
    w_near_other = other_core(w_near)

    halves = jnp.stack([tokens.reshape(2, half, width), cotangent.reshape(2, half, width)], axis=1)
    kept, got = pick(halves, core), other_core(pick(halves, 1 - core))
    mine = jnp.concatenate([kept[0], got[0], kept[1], got[1]], axis=1)
    body = 4 * width - LANES
    tail = lax.all_to_all(jnp.broadcast_to(mine[None, :, body:], (16, half, LANES)), Z, 0, 0, tiled=False)
    tail = tail.reshape(quarter, LANES)
    frames = lax.all_gather(mine[:, :body], Z, axis=0, tiled=True)
    w_far, frames, tail = lax.optimization_barrier((w_far, frames, tail))
    w_far_other = other_core(w_far)

    parts = forward_parts(frames, tail, w_near, w_far, w_near_other, w_far_other)
    parts, frames, tail = lax.optimization_barrier((parts, frames, tail))
    arrived = lax.all_to_all(parts.reshape(8, rows, 6 * units), PLANE, 0, 0, tiled=False)

    swap = other_core(jnp.concatenate([frames[:, width : 2 * width], frames[:, 3 * width :], tail], axis=1))
    token_pair = jnp.concatenate([frames[:, :width], swap[:, :width]])
    cot_pair = jnp.concatenate([frames[:, 2 * width : 3 * width], swap[:, width:]])
    hidden, kept, sent = plane_parts(arrived)
    hidden_own = lax.all_to_all(hidden, PLANE, 0, 0, tiled=False)

    got, hidden_own, token_far = lax.optimization_barrier((other_xh(sent), hidden_own, other_xh(token_pair)))
    grads_own = spread(jnp.stack([kept, got]), 8).reshape(8, 2, rows, 2 * units)

    hidden_own = hidden_own.reshape(quarter, 2 * units)
    hidden_other = other_core(hidden_own)
    w_down_pair = jnp.concatenate([w_near[2], w_far[2]])
    mixed = jnp.stack(
        [dot(hidden_own, w_down_pair).astype(BF16), dot(hidden_other, w_down_pair).astype(BF16)]
    )
    mixed = mixed.reshape(2, 16, half, width).transpose(1, 0, 2, 3).reshape(16, rows, width)
    mixed = halved(mixed, lax.axis_index("zn"), [(i, i ^ 1) for i in range(16)])
    units_pair = jnp.concatenate([hidden_own[:, :units], hidden_other[:, :units]])
    units_far = other_xh(jnp.concatenate([hidden_own[:, units:], hidden_other[:, units:]]))
    grads_own, mixed, cot_pair, units_far = lax.optimization_barrier((grads_own, mixed, cot_pair, units_far))
    cot_far = other_xh(cot_pair)
    grads_other = other_core(grads_own)
    landed = lax.all_to_all(mixed, ("zh", "zm"), 0, 0, tiled=False)
    grad_gate, grad_up = pair_grads(token_pair, token_far, grads_own, grads_other)
    landed, grad_gate, grad_up = lax.optimization_barrier((landed, grad_gate, grad_up))
    mixed = landed.astype(F32).sum(0).reshape(2, half, width)
    mixed = jnp.where(core == 0, mixed, mixed[::-1]).astype(BF16).reshape(rows, width)

    mixed, cot_far = lax.optimization_barrier((mixed, cot_far))

    grad_down = dot_tn(units_pair, cot_pair) + dot_tn(units_far, cot_far)
    return (mixed, grad_gate, grad_up, grad_down)


def solution(mesh):
    named = Mesh(mesh.devices.reshape(SIZES), SEQ + TP)
    return jax.shard_map(
        on_device,
        mesh=named,
        in_specs=(
            P(TP, SEQ),
            P(TP, SEQ),
            P(SEQ, TP),
            P(),
            P(SEQ, TP),
            P(),
            P(TP, SEQ),
            P(),
        ),
        out_specs=(P(TP, SEQ), P(SEQ, TP), P(SEQ, TP), P(TP, SEQ)),
        check_vma=False,
    )
```
